512 devices in a mesh: row: 16 (over z), col: 32 (over y, x, core).
Axes of the slice: x: 4, y: 4, z: 16, core: 2. Of those that a mesh axis runs over, the one named last changes fastest.
Arguments:
- rhs_above: float32 [32768, 4096], P('col', 'row'), may hold values from -6 to 6
- rhs_a: float32 [1024, 4096], P('col', 'row'), may hold values from -6 to 6
- rhs_b: float32 [1024, 4096], P('col', 'row'), may hold values from -6 to 6
- rows_a_above: float32 [1024, 32768], P('row', 'col'), may hold values from -0.1875 to 0.1875
- rows_b_above: float32 [1024, 32768], P('row', 'col'), may hold values from -0.1875 to 0.1875
- rows_b_a: float32 [1024, 1024], P('row', 'col'), may hold values from -0.1875 to 0.1875
- inverse_a: float32 [1024, 1024], P(None, 'col'), as said below
- inverse_b: float32 [1024, 1024], P(None, 'col'), as said below
Outputs:
- x_b: float32 [1024, 4096], P('col', 'row')
- x_a: float32 [1024, 4096], P('col', 'row')
- updated_above: float32 [32768, 4096], P('col', 'row')
The draws below stay inside these ranges and needn't reach their ends.
Inputs may be any that keep to these rules, and one draw needn't show every extreme that they name: inverse_a is lower triangular: zero above the diagonal, positive on it. inverse_b is lower triangular: zero above the diagonal, positive on it.
All inputs are finite; a program needn't handle non-finite values.
Results may differ from the reference program's by a relative error of at most 0.00012.
Values sent between devices are 32-bit elements; how exact they have to be, the bound alone decides.
No kernel may reach another device: no remote copies, remote signals or barrier semaphores. Data moves between devices by JAX's collectives and lax.ppermute only.
A program may use at most 64 MiB of HBM per device.

```python
import math
import jax
import jax.numpy as jnp
from jax import lax

PANEL = 1024
RHS = 4096
ABOVE = 32768


def assemble(diagonal, lower_part):
    index = jnp.arange(PANEL)
    strict = index[:, None] > index[None, :]
    same = index[:, None] == index[None, :]
    scaled = lower_part / math.sqrt(PANEL)
    return jnp.where(strict, scaled, 0.0) + jnp.where(same, diagonal[:, None], 0.0)


def draw_inverse_a(key, part):
    key = jax.random.fold_in(key, 11)
    first, second = jax.random.split(key)
    diagonal = jax.random.uniform(first, (PANEL,), jnp.float32, 0.5, 1.5)
    lower_part = jnp.clip(jax.random.normal(second, (PANEL, PANEL), jnp.float32), -4.0, 4.0)
    return assemble(diagonal, lower_part)


def draw_inverse_b(key, part):
    key = jax.random.fold_in(key, 12)
    first, second = jax.random.split(key)
    diagonal = jax.random.uniform(first, (PANEL,), jnp.float32, 0.5, 1.5)
    lower_part = jnp.clip(jax.random.normal(second, (PANEL, PANEL), jnp.float32), -4.0, 4.0)
    return assemble(diagonal, lower_part)


def level_of(stream_key, shape, pieces, smallest, largest):
    gain, own = 1.0, jax.random.fold_in(stream_key, 6)
    for position, blocks in pieces:
        heights = jnp.exp(jax.random.uniform(jax.random.fold_in(own, position), (blocks,), jnp.float32, smallest / len(pieces), largest / len(pieces)))
        gain = gain * jnp.repeat(heights, shape[position] // blocks).reshape([-1 if axis == position else 1 for axis in range(len(shape))])
    return gain


def gaussian(own_key, dims, spread, bound, shards=(), kind=jnp.bfloat16):
    values = spread * jax.random.normal(own_key, dims, jnp.float32)
    if shards:
        values = values * level_of(own_key, dims, shards, -0.22, 0.18)
    return jnp.clip(values, -bound, bound).astype(kind)


def setup_inputs(seed: int = 0) -> dict:
    keys = jax.random.split(jax.random.key(seed), 9)
    rhs_above = gaussian(keys[0], (ABOVE, RHS), 1.0, 6.0, ((0, 32), (1, 16)), jnp.float32)
    rhs_a = gaussian(keys[1], (PANEL, RHS), 1.0, 6.0, ((0, 32), (1, 16)), jnp.float32)
    rhs_b = gaussian(keys[2], (PANEL, RHS), 1.0, 6.0, ((0, 32), (1, 16)), jnp.float32)
    rows_a_above = gaussian(keys[3], (PANEL, ABOVE), PANEL ** -0.5, 0.1875, ((0, 16), (1, 32)), jnp.float32)
    rows_b_above = gaussian(keys[4], (PANEL, ABOVE), PANEL ** -0.5, 0.1875, ((0, 16), (1, 32)), jnp.float32)
    rows_b_a = gaussian(keys[5], (PANEL, PANEL), PANEL ** -0.5, 0.1875, ((0, 16), (1, 32)), jnp.float32)
    inverse_a = draw_inverse_a(jax.random.fold_in(keys[8], 71), 0)
    inverse_b = draw_inverse_b(jax.random.fold_in(keys[8], 71), 0)
    return dict(rhs_above=rhs_above, rhs_a=rhs_a, rhs_b=rhs_b, rows_a_above=rows_a_above, rows_b_above=rows_b_above, rows_b_a=rows_b_a, inverse_a=inverse_a, inverse_b=inverse_b)


def product(left, right):
    return lax.dot_general(left, right, (((0,), (0,)), ((), ())), precision=lax.Precision.HIGHEST, preferred_element_type=jnp.float32)


def reference(rhs_above, rhs_a, rhs_b, rows_a_above, rows_b_above, rows_b_a, inverse_a, inverse_b):
    x_b = product(inverse_b, rhs_b)
    coupled = rhs_a - product(rows_b_a, x_b)
    x_a = product(inverse_a, coupled)
    updated_above = rhs_above - product(rows_b_above, x_b) - product(rows_a_above, x_a)
    return x_b, x_a, updated_above
```

```python
import functools

import jax
import jax.numpy as jnp
from jax import lax
from jax.experimental import pallas as pl
from jax.experimental.pallas import tpu as pltpu
from jax.sharding import PartitionSpec as P

F32 = jnp.float32
BF16 = jnp.bfloat16
VMEM_LIMIT = 40 * 1024 * 1024


def split(a):
    high = a.astype(BF16)
    return high, (a - high.astype(F32)).astype(BF16)


def dot(a, b):
    return lax.dot_general(a, b, (((1,), (0,)), ((), ())), preferred_element_type=F32)


def product(a, b):
    a_high, a_low = split(a)
    b_high, b_low = split(b)
    return dot(a_high, b_high) + (dot(a_high, b_low) + dot(a_low, b_high))


def solve_kernel(planes, plane_ref, factor_ref, rhs_b_ref, rhs_a_ref, x_b_ref, x_a_ref, coupled_ref):
    step = pl.program_id(0)
    tile = 256
    panel, width = x_b_ref.shape
    steps = panel // tile
    shard = panel // factor_ref.shape[0]
    lines = panel // planes
    per_tile = tile // shard

    def factor():
        return factor_ref[...].reshape(panel, tile)

    def triangular(j, rhs, out_ref):
        height = tile * (j + 1)
        part = product(factor()[:height], rhs)
        if j:
            out_ref[: height - tile] += part[: height - tile]
        out_ref[height - tile : height] = part[height - tile :]

    for j in range(steps):

        @pl.when(step == j)
        def _(j=j):
            rhs = rhs_b_ref[j * per_tile : (j + 1) * per_tile].reshape(tile, width)
            triangular(j, rhs, x_b_ref)

        @pl.when(step == steps + j)
        def _(j=j):
            blocks = []
            for i in range(tile // lines):
                block = lax.rem(plane_ref[0] + j * (tile // lines) + i, panel // lines)
                blocks.append(x_b_ref[pl.ds(pl.multiple_of(block * lines, lines), lines), :])
            part = product(factor(), jnp.concatenate(blocks, axis=0))
            before = coupled_ref[...] if j else rhs_a_ref[...].reshape(panel, width)
            coupled_ref[...] = before - part

        @pl.when(step == 2 * steps + j)
        def _(j=j):
            triangular(j, coupled_ref[j * tile : (j + 1) * tile], x_a_ref)


def solve(plane, gathered, panel, width, planes):
    shards, rows, tile = gathered.shape
    shard = panel // shards
    block = (shards, shard, tile)
    steps = 3 * panel // tile
    return pl.pallas_call(
        functools.partial(solve_kernel, planes),
        grid=(steps,),
        out_shape=[jax.ShapeDtypeStruct((panel, width), F32)] * 2,
        in_specs=[
            pl.BlockSpec(memory_space=pltpu.SMEM),
            pl.BlockSpec(block, lambda s: (0, s, 0)),
            pl.BlockSpec(block, lambda s: (0, steps, 0)),
            pl.BlockSpec(block, lambda s: (0, steps + 1, 0)),
        ],
        out_specs=[pl.BlockSpec((panel, width), lambda s: (0, 0))] * 2,
        scratch_shapes=[pltpu.VMEM((panel, width), F32)],
        compiler_params=pltpu.CompilerParams(vmem_limit_bytes=VMEM_LIMIT),
        name="solve",
    )(plane, gathered, gathered, gathered)


def update_kernel(offsets, plane_ref, x_b_ref, x_a_ref, rhs_ref, *refs):
    chunks, out_ref, high, low = refs[:-3], refs[-3], refs[-2], refs[-1]
    lines = chunks[0].shape[0] // 2
    planes = x_b_ref.shape[0] // lines
    depth = 2 * lines

    @pl.when(pl.program_id(0) == 0)
    def _():
        for n, offset in enumerate(offsets):
            block = lax.rem(plane_ref[0] + offset, planes)
            rows = pl.ds(pl.multiple_of(block * lines, lines), lines)
            x = jnp.concatenate([x_b_ref[rows, :], x_a_ref[rows, :]], axis=0).T
            x_high, x_low = split(x)
            high[:, n * depth : (n + 1) * depth] = x_high
            low[:, n * depth : (n + 1) * depth] = x_low

    total = None
    n = 0
    while n < len(chunks):
        pair = chunks[n : n + 2]
        rows = jnp.concatenate([c[...] for c in pair], axis=0) if len(pair) > 1 else pair[0][...]
        l_high, l_low = split(rows)
        lanes = slice(n * depth, (n + len(pair)) * depth)
        part = dot(high[:, lanes], l_high) + (dot(low[:, lanes], l_high) + dot(high[:, lanes], l_low))
        total = part if total is None else total + part
        n += len(pair)
    out_ref[...] = rhs_ref[...] - total.T


def update(plane, x_b, x_a, rhs, chunks, offsets, name):
    height, width = rhs.shape
    panel = x_b.shape[0]
    tile = 256
    depth = sum(c.shape[0] for c in chunks)
    whole = pl.BlockSpec((panel, width), lambda n: (0, 0))
    rows = pl.BlockSpec((tile, width), lambda n: (n, 0))

    return pl.pallas_call(
        functools.partial(update_kernel, offsets),
        grid=(height // tile,),
        out_shape=jax.ShapeDtypeStruct((height, width), F32),
        in_specs=[pl.BlockSpec(memory_space=pltpu.SMEM), whole, whole, rows]
        + [pl.BlockSpec((c.shape[0], tile), lambda n: (0, n)) for c in chunks],
        out_specs=rows,
        scratch_shapes=[pltpu.VMEM((width, depth), BF16)] * 2,
        compiler_params=pltpu.CompilerParams(vmem_limit_bytes=VMEM_LIMIT),
        name=name,
    )(plane, x_b, x_a, rhs, *chunks)


def shift(planes, by):
    return [(i, (i + by) % planes) for i in range(planes)]


def collect(block, planes):
    distance = 1
    while distance < planes:
        block = jnp.concatenate([block, lax.ppermute(block, "row", shift(planes, -distance))], axis=0)
        distance *= 2
    return block


def tiles(a, width):
    return [a[:, i : i + width] for i in range(0, a.shape[1], width)]


def make(planes):
    def shards(rhs_above, rhs_a, rhs_b, rows_a_above, rows_b_above, rows_b_a, inverse_a, inverse_b):
        width = rhs_b.shape[1]
        panel = inverse_b.shape[0]
        plane = lax.axis_index("row").astype(jnp.int32).reshape(1)
        column = lax.axis_index("col")

        across = collect(rows_b_a.T[None], planes)
        across = across.transpose(1, 0, 2).reshape(rhs_b.shape[0], panel)
        packed = jnp.concatenate(
            tiles(inverse_b.T, width) + tiles(across, width) + tiles(inverse_a.T, width) + [rhs_b, rhs_a], axis=0
        )
        gathered = lax.all_gather(packed, "col", axis=0)

        own = jnp.concatenate([rows_b_above, rows_a_above], axis=0)
        up = down = own
        chunks, offsets = [own], [0]
        half = planes // 2
        for step in range(1, half):
            up = lax.ppermute(up, "row", shift(planes, 1))
            down = lax.ppermute(down, "row", shift(planes, -1))
            chunks += [up, down]
            offsets += [planes - step, step]
        middle = own.shape[0] // 2
        last = [
            lax.ppermute(up[:middle], "row", shift(planes, 1)),
            lax.ppermute(down[middle:], "row", shift(planes, -1)),
        ]

        x_b, x_a = solve(plane, gathered, panel, width, planes)
        partial = update(plane, x_b, x_a, rhs_above, chunks, offsets, "update_near")
        far = jnp.concatenate(last, axis=0)
        updated = update(plane, x_b, x_a, partial, [far], [half], "update_far")
        first = column * rhs_b.shape[0]
        return (
            lax.dynamic_slice_in_dim(x_b, first, rhs_b.shape[0], 0),
            lax.dynamic_slice_in_dim(x_a, first, rhs_b.shape[0], 0),
            updated,
        )

    return shards


def solution(mesh):
    in_specs = (
        P("col", "row"),
        P("col", "row"),
        P("col", "row"),
        P("row", "col"),
        P("row", "col"),
        P("row", "col"),
        P(None, "col"),
        P(None, "col"),
    )
    out_specs = (P("col", "row"), P("col", "row"), P("col", "row"))
    return jax.shard_map(
        make(mesh.shape["row"]), mesh=mesh, in_specs=in_specs, out_specs=out_specs, check_vma=False
    )
```

```python
import functools

import jax
import jax.numpy as jnp
from jax import lax
from jax.experimental import pallas as pl
from jax.experimental.pallas import tpu as pltpu
from jax.sharding import PartitionSpec as P

F32 = jnp.float32
BF16 = jnp.bfloat16
VMEM_LIMIT = 20 * 1024 * 1024
UPDATE_LIMIT = 56 * 1024 * 1024


def split(a):
    high = a.astype(BF16)
    return high, (a - high.astype(F32)).astype(BF16)


def dot(a, b):
    return lax.dot_general(a, b, (((1,), (0,)), ((), ())), preferred_element_type=F32)


def product(a, b):
    a_high, a_low = split(a)
    b_high, b_low = split(b)
    return dot(a_high, b_high) + (dot(a_high, b_low) + dot(a_low, b_high))


def call(kernel, shapes, args, after=()):
    vmem = pl.BlockSpec(memory_space=pltpu.VMEM)

    def body(*refs):
        kernel(*refs[: len(args)], *refs[len(args) + len(after) :])

    return pl.pallas_call(
        body,
        out_shape=[jax.ShapeDtypeStruct(*s) for s in shapes],
        in_specs=[vmem] * len(args) + [pl.BlockSpec(memory_space=pl.ANY)] * len(after),
        out_specs=[vmem] * len(shapes),
        compiler_params=pltpu.CompilerParams(vmem_limit_bytes=VMEM_LIMIT),
        name=kernel.__name__,
    )(*args, *after)


def copy_out(copies_ref, block):
    for i in range(copies_ref.shape[0]):
        copies_ref[i] = block


def begin(across_ref, rows_b_ref, rows_a_ref, across_copies_ref, own_ref):
    half = across_ref.shape[0] // 2
    copy_out(across_copies_ref, jnp.concatenate([across_ref[:half, :], across_ref[half:, :]], axis=1))
    lines = rows_b_ref.shape[0]
    own_ref[:lines, :] = rows_b_ref[...]
    own_ref[lines:, :] = rows_a_ref[...]


def send(block_ref, copies_ref):
    copy_out(copies_ref, block_ref[...])


def solve(inverse_ref, rhs_ref, x_ref, copies_ref):
    panel, width = inverse_ref.shape[1], x_ref.shape[1]
    x = product(inverse_ref[...], rhs_ref[...].reshape(panel, width))
    x_ref[...] = x
    copy_out(copies_ref, x)


def couple(rhs_ref, across_ref, x_ref, copies_ref):
    planes, _, lanes = across_ref.shape
    lines = lanes // 2
    parts = [across_ref[z] for z in range(planes)]
    parts = [jnp.concatenate([p[:, :lines], p[:, lines:]], axis=0) for p in parts]
    width = rhs_ref.shape[1]
    x = x_ref[...].reshape(planes * lines, width)
    copy_out(copies_ref, rhs_ref[...] - product(jnp.concatenate(parts, axis=1), x))


def update_kernel(planes, sources, plane_ref, x_b_ref, x_a_ref, rhs_ref, *refs):
    row_refs, (out_ref, x_ref, high, low) = refs[:-4], refs[-4:]
    shards, shard, width = x_b_ref.shape
    lines = shards * shard // planes
    tile = 256
    depth = x_ref.shape[0]

    @pl.when(pl.program_id(0) == 0)
    def _():
        x = [r.reshape(shards * shard, width) for r in (x_b_ref, x_a_ref)]
        for n, (panel, offset) in enumerate(sources):
            place = lax.rem(plane_ref[0] + offset, planes)
            x_ref[n * lines : (n + 1) * lines] = x[panel][pl.ds(pl.multiple_of(place * lines, lines), lines), :]
        for k in range(0, depth, tile):
            x_high, x_low = split(x_ref[k : min(k + tile, depth)].T)
            high[:, k : k + tile] = x_high
            low[:, k : k + tile] = x_low

    total = None
    for k in range(0, depth, tile):
        pieces = row_refs[k // lines : (k + tile) // lines]
        l_high, l_low = split(jnp.concatenate([r[...] for r in pieces], axis=0))
        lanes = slice(k, k + l_high.shape[0])
        part = dot(high[:, lanes], l_high) + (dot(low[:, lanes], l_high) + dot(high[:, lanes], l_low))
        total = part if total is None else total + part
    out_ref[...] = rhs_ref[...] - total.T


def update(plane, x_b, x_a, rhs, blocks, sources, planes, name):
    height, width = rhs.shape
    tile = 256
    shards, shard, _ = x_b.shape
    lines = shards * shard // planes
    whole = pl.BlockSpec(x_b.shape, lambda n: (0, 0, 0))
    out = pl.BlockSpec((tile, width), lambda n: (n, 0))
    rows, specs = [], []
    for r, half in blocks:
        rows.append(r)
        specs.append(pl.BlockSpec((lines, tile), lambda n, half=half: (half, n)))
    depth = lines * len(sources)
    return pl.pallas_call(
        functools.partial(update_kernel, planes, tuple(sources)),
        grid=(height // tile,),
        out_shape=jax.ShapeDtypeStruct((height, width), F32),
        in_specs=[pl.BlockSpec(memory_space=pltpu.SMEM), whole, whole, out] + specs,
        out_specs=out,
        scratch_shapes=[pltpu.VMEM((depth, width), F32)] + [pltpu.VMEM((width, depth), BF16)] * 2,
        compiler_params=pltpu.CompilerParams(vmem_limit_bytes=UPDATE_LIMIT),
        name=name,
    )(plane, x_b, x_a, rhs, *rows)


def exchange(copies, axis):
    return lax.all_to_all(copies, axis, 0, 0, tiled=True)


def ring(own, planes):
    def move(block, by):
        return lax.ppermute(block, "row", [(i, (i + by) % planes) for i in range(planes)])

    up = down = own
    blocks, offsets = [own], [0]
    half = planes // 2
    for step in range(1, half):
        up, down = move(up, 1), move(down, -1)
        blocks += [up, down]
        offsets += [planes - step, step]
    middle = own.shape[0] // 2
    blocks += [move(up[:middle], 1), move(down[middle:], -1)]
    offsets += [half]
    return blocks, tuple(offsets)


def make(planes, columns):
    def shards(rhs_above, rhs_a, rhs_b, rows_a_above, rows_b_above, rows_b_a, inverse_a, inverse_b):
        shard, width = rhs_b.shape
        lines, height = rows_b_above.shape
        plane = lax.axis_index("row").astype(jnp.int32).reshape(1)
        local = ((shard, width), F32)
        copies = ((columns, shard, width), F32)

        across_copies, own = call(
            begin,
            [((planes, shard // 2, 2 * lines), F32), ((2 * lines, height), F32)],
            [rows_b_a.T, rows_b_above, rows_a_above],
        )
        blocks, offsets = ring(own, planes)
        across = exchange(across_copies, "row")
        (rhs_copies,) = call(send, [copies], [rhs_b])
        x_b, x_copies = call(solve, [local, copies], [inverse_b.T, exchange(rhs_copies, "col")], after=blocks[1:3])
        x_b_all = exchange(x_copies, "col")
        (coupled,) = call(couple, [copies], [rhs_a, across, x_b_all], after=blocks[5:7])
        x_a, x_copies = call(solve, [local, copies], [inverse_a.T, exchange(coupled, "col")], after=blocks[9:11])
        x_a_all = exchange(x_copies, "col")

        near, offsets = offsets[:-1], offsets[-1]
        whole, halves = blocks[:-2], blocks[-2:]
        partial = update(
            plane, x_b_all, x_b_all, rhs_above, [(r, 0) for r in whole], [(0, z) for z in near], planes, "update_b"
        )
        updated = update(
            plane,
            x_b_all,
            x_a_all,
            partial,
            [(r, 1) for r in whole] + [(r, 0) for r in halves],
            [(1, z) for z in near] + [(0, offsets), (1, offsets)],
            planes,
            "update_a",
        )
        return x_b, x_a, updated

    return shards


def solution(mesh):
    in_specs = (
        P("col", "row"),
        P("col", "row"),
        P("col", "row"),
        P("row", "col"),
        P("row", "col"),
        P("row", "col"),
        P(None, "col"),
        P(None, "col"),
    )
    out_specs = (P("col", "row"), P("col", "row"), P("col", "row"))
    return jax.shard_map(
        make(mesh.shape["row"], mesh.shape["col"]),
        mesh=mesh,
        in_specs=in_specs,
        out_specs=out_specs,
        check_vma=False,
    )
```

```python
import functools

import jax
import jax.numpy as jnp
from jax import lax
from jax.experimental import pallas as pl
from jax.experimental.pallas import tpu as pltpu
from jax.sharding import PartitionSpec as P

F32 = jnp.float32
BF16 = jnp.bfloat16
VMEM_LIMIT = 20 * 1024 * 1024
UPDATE_LIMIT = 56 * 1024 * 1024


def split(a):
    high = a.astype(BF16)
    return high, (a - high.astype(F32)).astype(BF16)


def dot(a, b):
    return lax.dot_general(a, b, (((1,), (0,)), ((), ())), preferred_element_type=F32)


def product(a, b):
    a_high, a_low = split(a)
    b_high, b_low = split(b)
    return dot(a_high, b_high) + (dot(a_high, b_low) + dot(a_low, b_high))


def call(kernel, shapes, args, after=(), scratch=()):
    vmem = pl.BlockSpec(memory_space=pltpu.VMEM)
    smem = pl.BlockSpec(memory_space=pltpu.SMEM)

    def body(*refs):
        kernel(*refs[: len(args)], *refs[len(args) + len(after) :])

    return pl.pallas_call(
        body,
        out_shape=[jax.ShapeDtypeStruct(s, F32) for s in shapes],
        in_specs=[smem if a.dtype == jnp.int32 else vmem for a in args] + [pl.BlockSpec(memory_space=pl.ANY)] * len(after),
        out_specs=[vmem] * len(shapes),
        scratch_shapes=[pltpu.VMEM(s, F32) for s in scratch],
        compiler_params=pltpu.CompilerParams(vmem_limit_bytes=VMEM_LIMIT),
        name=kernel.__name__,
    )(*args, *after)


def copy_out(copies_ref, block):
    for i in range(copies_ref.shape[0]):
        copies_ref[i] = block


def begin(across_ref, copies_ref):
    half = across_ref.shape[0] // 2
    copy_out(copies_ref, jnp.concatenate([across_ref[:half, :], across_ref[half:, :]], axis=1))


def join(rows_b_ref, rows_a_ref, own_ref):
    lines = rows_b_ref.shape[0]
    own_ref[:lines, :] = rows_b_ref[...]
    own_ref[lines:, :] = rows_a_ref[...]


def send(block_ref, copies_ref):
    copy_out(copies_ref, block_ref[...])


def merge(core, same, other, whole_ref):
    whole_ref[:, pl.ds(core, 1)] = same[...][:, None]
    whole_ref[:, pl.ds(1 - core, 1)] = other[...][:, None]
    chips, cores, shard, width = whole_ref.shape
    return whole_ref[...].reshape(chips * cores * shard, width)


def solve(core_ref, inverse_ref, same_ref, other_ref, x_ref, copies_ref, whole_ref):
    x = product(inverse_ref[...], merge(core_ref[0], same_ref, other_ref, whole_ref))
    x_ref[...] = x
    copy_out(copies_ref, x)


def couple(core_ref, rhs_ref, across_ref, same_ref, other_ref, copies_ref, whole_ref):
    planes, _, lanes = across_ref.shape
    lines = lanes // 2
    parts = [across_ref[z] for z in range(planes)]
    parts = [jnp.concatenate([p[:, :lines], p[:, lines:]], axis=0) for p in parts]
    x = merge(core_ref[0], same_ref, other_ref, whole_ref)
    copy_out(copies_ref, rhs_ref[...] - product(jnp.concatenate(parts, axis=1), x))


def gather_x(refs, place, core, out_ref, at):
    for same, other in refs:
        shard = same.shape[-2]
        out_ref[pl.ds(pl.multiple_of(at + core * shard, shard), shard), :] = same[place]
        out_ref[pl.ds(pl.multiple_of(at + (1 - core) * shard, shard), shard), :] = other[place]
        at += 2 * shard


def near_kernel(planes, offsets, plane_ref, core_ref, b_same, b_other, a_same, a_other, rhs_ref, *refs):
    count = len(offsets)
    row_refs, (out_ref, x_ref, rows_ref, total_ref, semaphores) = refs[:count], refs[count:]
    block = rows_ref.shape[1]
    copies = [pltpu.make_async_copy(r, rows_ref.at[n], semaphores.at[n]) for n, r in enumerate(row_refs)]
    for copy in copies:
        copy.start()
    for n, offset in enumerate(offsets):
        place = lax.rem(plane_ref[0] + offset, planes)
        gather_x(((b_same, b_other), (a_same, a_other)), place, core_ref[0], x_ref, n * block)
    for n in range(0, count, 2):
        last = min(n + 2, count)
        for copy in copies[n:last]:
            copy.wait()
        rows = rows_ref[n:last].reshape((last - n) * block, rows_ref.shape[2])
        part = product(x_ref[n * block : last * block].T, rows)
        total_ref[...] = part if n == 0 else total_ref[...] + part
    out_ref[...] = rhs_ref[...] - total_ref[...].T


def update_near(plane, core, x, rhs, blocks, offsets, planes):
    height, width = rhs.shape
    vmem, smem = pl.BlockSpec(memory_space=pltpu.VMEM), pl.BlockSpec(memory_space=pltpu.SMEM)
    count, block = len(blocks), blocks[0].shape[0]
    return pl.pallas_call(
        functools.partial(near_kernel, planes, offsets),
        out_shape=jax.ShapeDtypeStruct((height, width), F32),
        in_specs=[smem] * 2 + [vmem] * (len(x) + 1) + [pl.BlockSpec(memory_space=pl.ANY)] * count,
        out_specs=vmem,
        scratch_shapes=[
            pltpu.VMEM((count * block, width), F32),
            pltpu.VMEM((count, block, height), F32),
            pltpu.VMEM((width, height), F32),
            pltpu.SemaphoreType.DMA((count,)),
        ],
        compiler_params=pltpu.CompilerParams(vmem_limit_bytes=UPDATE_LIMIT),
        name="update_near",
    )(plane, core, *x, rhs, *blocks)


def far_kernel(planes, plane_ref, core_ref, b_same, b_other, a_same, a_other, rhs_ref, rows_b_ref, rows_a_ref, out_ref, x_ref):
    place = lax.rem(plane_ref[0] + planes // 2, planes)
    gather_x(((b_same, b_other), (a_same, a_other)), place, core_ref[0], x_ref, 0)
    rows = jnp.concatenate([rows_b_ref[...], rows_a_ref[...]], axis=0)
    out_ref[...] = rhs_ref[...] - product(x_ref[...].T, rows).T


def update_far(plane, core, x, rhs, blocks, planes):
    height, width = rhs.shape
    tile = 512
    smem = pl.BlockSpec(memory_space=pltpu.SMEM)
    out = pl.BlockSpec((tile, width), lambda n: (n, 0))
    return pl.pallas_call(
        functools.partial(far_kernel, planes),
        grid=(height // tile,),
        out_shape=jax.ShapeDtypeStruct((height, width), F32),
        in_specs=[smem] * 2
        + [pl.BlockSpec(a.shape, lambda n: (0, 0, 0)) for a in x]
        + [out]
        + [pl.BlockSpec((b.shape[0], tile), lambda n: (0, n)) for b in blocks],
        out_specs=out,
        scratch_shapes=[pltpu.VMEM((sum(b.shape[0] for b in blocks), width), F32)],
        compiler_params=pltpu.CompilerParams(vmem_limit_bytes=VMEM_LIMIT),
        name="update_far",
    )(plane, core, *x, rhs, *blocks)


def exchange(copies, axis):
    return lax.all_to_all(copies, axis, 0, 0, tiled=True)


def spread(copies):
    same = exchange(copies, "chip")
    return same, lax.ppermute(same, "core", [(0, 1), (1, 0)])


def ring(own, planes):
    def move(block, by):
        return lax.ppermute(block, "row", [(i, (i + by) % planes) for i in range(planes)])

    up = down = own
    blocks, offsets = [own], [0]
    half = planes // 2
    for step in range(1, half):
        up, down = move(up, 1), move(down, -1)
        blocks += [up, down]
        offsets += [planes - step, step]
    middle = own.shape[0] // 2
    blocks += [move(up[:middle], 1), move(down[middle:], -1)]
    offsets += [half]
    return blocks, tuple(offsets)


def make(planes, chips):
    def shards(rhs_above, rhs_a, rhs_b, rows_a_above, rows_b_above, rows_b_a, inverse_a, inverse_b):
        shard, width = rhs_b.shape
        lines, height = rows_b_above.shape
        plane, core = (lax.axis_index(a).astype(jnp.int32).reshape(1) for a in ("row", "core"))
        local, copies, whole = (shard, width), (chips, shard, width), (chips, 2, shard, width)

        (across_copies,) = call(begin, [(planes, shard // 2, 2 * lines)], [rows_b_a.T])
        across = exchange(across_copies, "row")
        (own,) = call(join, [(2 * lines, height)], [rows_b_above, rows_a_above])
        blocks, offsets = ring(own, planes)
        (rhs_copies,) = call(send, [copies], [rhs_b])
        x_b, x_copies = call(
            solve, [local, copies], [core, inverse_b.T, *spread(rhs_copies)], after=blocks[1:3] + [across], scratch=[whole]
        )
        x_b_all = spread(x_copies)
        (coupled,) = call(
            couple, [copies], [core, rhs_a, across, *x_b_all], after=blocks[5:7], scratch=[whole]
        )
        x_a, x_copies = call(
            solve, [local, copies], [core, inverse_a.T, *spread(coupled)], after=blocks[9:11], scratch=[whole]
        )
        x = x_b_all + spread(x_copies)
        partial = update_near(plane, core, x, rhs_above, blocks[:-2], offsets[:-1], planes)
        return x_b, x_a, update_far(plane, core, x, partial, blocks[-2:], planes)

    return shards


def solution(mesh):
    planes, columns = mesh.shape["row"], mesh.shape["col"]
    mesh = jax.sharding.Mesh(mesh.devices.reshape(planes, columns // 2, 2), ("row", "chip", "core"))
    column = ("chip", "core")
    in_specs = (
        P(column, "row"),
        P(column, "row"),
        P(column, "row"),
        P("row", column),
        P("row", column),
        P("row", column),
        P(None, column),
        P(None, column),
    )
    out_specs = (P(column, "row"), P(column, "row"), P(column, "row"))
    return jax.shard_map(
        make(planes, columns // 2), mesh=mesh, in_specs=in_specs, out_specs=out_specs, check_vma=False
    )
```

```python
import functools

import jax
import jax.numpy as jnp
from jax import lax
from jax.experimental import pallas as pl
from jax.experimental.pallas import tpu as pltpu
from jax.sharding import PartitionSpec as P

F32 = jnp.float32
BF16 = jnp.bfloat16
VMEM_LIMIT = 20 * 1024 * 1024
UPDATE_LIMIT = 56 * 1024 * 1024


def split(a):
    high = a.astype(BF16)
    return high, (a - high.astype(F32)).astype(BF16)


def dot(a, b):
    return lax.dot_general(a, b, (((1,), (0,)), ((), ())), preferred_element_type=F32)


def product(a, b):
    a_high, a_low = split(a)
    b_high, b_low = split(b)
    return dot(a_high, b_high) + (dot(a_high, b_low) + dot(a_low, b_high))


def call(kernel, shapes, args, after=(), scratch=()):
    vmem = pl.BlockSpec(memory_space=pltpu.VMEM)
    smem = pl.BlockSpec(memory_space=pltpu.SMEM)

    def body(*refs):
        kernel(*refs[: len(args)], *refs[len(args) + len(after) :])

    return pl.pallas_call(
        body,
        out_shape=[jax.ShapeDtypeStruct(s, F32) for s in shapes],
        in_specs=[smem if a.dtype == jnp.int32 else vmem for a in args] + [pl.BlockSpec(memory_space=pl.ANY)] * len(after),
        out_specs=[vmem] * len(shapes),
        scratch_shapes=[pltpu.VMEM(s, F32) for s in scratch],
        compiler_params=pltpu.CompilerParams(vmem_limit_bytes=VMEM_LIMIT),
        name=kernel.__name__,
    )(*args, *after)


def copy_out(copies_ref, block):
    for i in range(copies_ref.shape[0]):
        copies_ref[i] = block


def begin(across_ref, copies_ref):
    half = across_ref.shape[0] // 2
    copy_out(copies_ref, jnp.concatenate([across_ref[:half, :], across_ref[half:, :]], axis=1))


def join(rows_b_ref, rows_a_ref, own_ref):
    lines = rows_b_ref.shape[0]
    own_ref[:lines, :] = rows_b_ref[...]
    own_ref[lines:, :] = rows_a_ref[...]


def send(block_ref, copies_ref):
    copy_out(copies_ref, block_ref[...])


def merge(core, same, other, whole_ref):
    whole_ref[:, pl.ds(core, 1)] = same[...][:, None]
    whole_ref[:, pl.ds(1 - core, 1)] = other[...][:, None]
    chips, cores, shard, width = whole_ref.shape
    return whole_ref[...].reshape(chips * cores * shard, width)


def solve(core_ref, inverse_ref, same_ref, other_ref, x_ref, copies_ref, whole_ref):
    x = product(inverse_ref[...], merge(core_ref[0], same_ref, other_ref, whole_ref))
    x_ref[...] = x
    copy_out(copies_ref, x)


def couple(core_ref, rhs_ref, across_ref, same_ref, other_ref, copies_ref, whole_ref):
    planes, _, lanes = across_ref.shape
    lines = lanes // 2
    parts = [across_ref[z] for z in range(planes)]
    parts = [jnp.concatenate([p[:, :lines], p[:, lines:]], axis=0) for p in parts]
    x = merge(core_ref[0], same_ref, other_ref, whole_ref)
    copy_out(copies_ref, rhs_ref[...] - product(jnp.concatenate(parts, axis=1), x))


def gather_x(refs, place, core, out_ref, at):
    for same, other in refs:
        shard = same.shape[-2]
        out_ref[pl.ds(pl.multiple_of(at + core * shard, shard), shard), :] = same[place]
        out_ref[pl.ds(pl.multiple_of(at + (1 - core) * shard, shard), shard), :] = other[place]
        at += 2 * shard


def near_kernel(planes, offsets, plane_ref, core_ref, b_same, b_other, a_same, a_other, rhs_ref, *refs):
    count = len(offsets)
    row_refs, (out_ref, x_ref, rows_ref, total_ref, semaphores) = refs[:count], refs[count:]
    block = rows_ref.shape[1]
    copies = [pltpu.make_async_copy(r, rows_ref.at[n], semaphores.at[n]) for n, r in enumerate(row_refs)]
    for copy in copies:
        copy.start()
    for n, offset in enumerate(offsets):
        place = lax.rem(plane_ref[0] + offset, planes)
        gather_x(((b_same, b_other), (a_same, a_other)), place, core_ref[0], x_ref, n * block)
    for n in range(0, count, 2):
        last = min(n + 2, count)
        for copy in copies[n:last]:
            copy.wait()
        rows = rows_ref[n:last].reshape((last - n) * block, rows_ref.shape[2])
        part = product(x_ref[n * block : last * block].T, rows)
        total_ref[...] = part if n == 0 else total_ref[...] + part
    out_ref[...] = rhs_ref[...] - total_ref[...].T


def update_near(plane, core, x, rhs, blocks, offsets, planes):
    height, width = rhs.shape
    vmem, smem = pl.BlockSpec(memory_space=pltpu.VMEM), pl.BlockSpec(memory_space=pltpu.SMEM)
    count, block = len(blocks), blocks[0].shape[0]
    return pl.pallas_call(
        functools.partial(near_kernel, planes, offsets),
        out_shape=jax.ShapeDtypeStruct((height, width), F32),
        in_specs=[smem] * 2 + [vmem] * (len(x) + 1) + [pl.BlockSpec(memory_space=pl.ANY)] * count,
        out_specs=vmem,
        scratch_shapes=[
            pltpu.VMEM((count * block, width), F32),
            pltpu.VMEM((count, block, height), F32),
            pltpu.VMEM((width, height), F32),
            pltpu.SemaphoreType.DMA((count,)),
        ],
        compiler_params=pltpu.CompilerParams(vmem_limit_bytes=UPDATE_LIMIT),
        name="update_near",
    )(plane, core, *x, rhs, *blocks)


def far_kernel(planes, plane_ref, core_ref, *refs):
    x_refs, rhs_in, row_refs = refs[:4], refs[4], refs[5:-6]
    out_ref, parts_ref, x_ref, rhs_ref, rows_ref, semaphores = refs[-6:]
    place = lax.rem(plane_ref[0] + planes // 2, planes)
    lines = row_refs[0].shape[0]
    pairs = [(r.at[pl.ds(place, 1)], parts_ref.at[pl.ds(n, 1)]) for n, r in enumerate(x_refs)]
    pairs += [(r, rows_ref.at[pl.ds(n * lines, lines)]) for n, r in enumerate(row_refs)] + [(rhs_in, rhs_ref)]
    copies = [pltpu.make_async_copy(*pair, semaphores.at[n]) for n, pair in enumerate(pairs)]
    for copy in copies:
        copy.start()
    for copy in copies[:-1]:
        copy.wait()
    parts = [parts_ref.at[pl.ds(n, 1)] for n in range(4)]
    gather_x((parts[:2], parts[2:]), 0, core_ref[0], x_ref, 0)
    part = product(x_ref[...].T, rows_ref[...]).T
    copies[-1].wait()
    out_ref[...] = rhs_ref[...] - part


def update_far(plane, core, x, rhs, blocks, planes):
    vmem, smem, whole = (pl.BlockSpec(memory_space=m) for m in (pltpu.VMEM, pltpu.SMEM, pl.ANY))
    height, width = rhs.shape
    depth = sum(b.shape[0] for b in blocks)
    return pl.pallas_call(
        functools.partial(far_kernel, planes),
        out_shape=jax.ShapeDtypeStruct(rhs.shape, F32),
        in_specs=[smem] * 2 + [whole] * (len(x) + 1 + len(blocks)),
        out_specs=vmem,
        scratch_shapes=[
            pltpu.VMEM((len(x),) + x[0].shape[1:], F32),
            pltpu.VMEM((depth, width), F32),
            pltpu.VMEM(rhs.shape, F32),
            pltpu.VMEM((depth, height), F32),
            pltpu.SemaphoreType.DMA((len(x) + len(blocks) + 1,)),
        ],
        compiler_params=pltpu.CompilerParams(vmem_limit_bytes=UPDATE_LIMIT),
        name="update_far",
    )(plane, core, *x, rhs, *blocks)


def exchange(copies, axis):
    return lax.all_to_all(copies, axis, 0, 0, tiled=True)


def spread(copies):
    same = exchange(copies, "chip")
    return same, lax.ppermute(same, "core", [(0, 1), (1, 0)])


def ring(own, planes):
    def move(block, by):
        return lax.ppermute(block, "row", [(i, (i + by) % planes) for i in range(planes)])

    up = down = own
    blocks, offsets = [own], [0]
    half = planes // 2
    for step in range(1, half):
        up, down = move(up, 1), move(down, -1)
        blocks += [up, down]
        offsets += [planes - step, step]
    middle = own.shape[0] // 2
    blocks += [move(up[:middle], 1), move(down[middle:], -1)]
    offsets += [half]
    return blocks, tuple(offsets)


def make(planes, chips):
    def shards(rhs_above, rhs_a, rhs_b, rows_a_above, rows_b_above, rows_b_a, inverse_a, inverse_b):
        shard, width = rhs_b.shape
        lines, height = rows_b_above.shape
        plane, core = (lax.axis_index(a).astype(jnp.int32).reshape(1) for a in ("row", "core"))
        local, copies, whole = (shard, width), (chips, shard, width), (chips, 2, shard, width)

        (across_copies,) = call(begin, [(planes, shard // 2, 2 * lines)], [rows_b_a.T])
        across = exchange(across_copies, "row")
        (own,) = call(join, [(2 * lines, height)], [rows_b_above, rows_a_above])
        blocks, offsets = ring(own, planes)
        (rhs_copies,) = call(send, [copies], [rhs_b])
        x_b, x_copies = call(
            solve, [local, copies], [core, inverse_b.T, *spread(rhs_copies)], after=blocks[1:2] + [across], scratch=[whole]
        )
        x_b_all = spread(x_copies)
        (coupled,) = call(
            couple, [copies], [core, rhs_a, across, *x_b_all], after=blocks[5:6], scratch=[whole]
        )
        x_a, x_copies = call(
            solve, [local, copies], [core, inverse_a.T, *spread(coupled)], after=blocks[9:10], scratch=[whole]
        )
        x = x_b_all + spread(x_copies)
        partial = update_near(plane, core, x, rhs_above, blocks[:-2], offsets[:-1], planes)
        return x_b, x_a, update_far(plane, core, x, partial, blocks[-2:], planes)

    return shards


def solution(mesh):
    planes, columns = mesh.shape["row"], mesh.shape["col"]
    mesh = jax.sharding.Mesh(mesh.devices.reshape(planes, columns // 2, 2), ("row", "chip", "core"))
    column = ("chip", "core")
    in_specs = (
        P(column, "row"),
        P(column, "row"),
        P(column, "row"),
        P("row", column),
        P("row", column),
        P("row", column),
        P(None, column),
        P(None, column),
    )
    out_specs = (P(column, "row"), P(column, "row"), P(column, "row"))
    return jax.shard_map(
        make(planes, columns // 2), mesh=mesh, in_specs=in_specs, out_specs=out_specs, check_vma=False
    )
```

```python
import functools

import jax
import jax.numpy as jnp
from jax import lax
from jax.experimental import pallas as pl
from jax.experimental.pallas import tpu as pltpu
from jax.sharding import PartitionSpec as P

F32 = jnp.float32
BF16 = jnp.bfloat16
VMEM_LIMIT = 20 * 1024 * 1024
UPDATE_LIMIT = 56 * 1024 * 1024


def split(a):
    high = a.astype(BF16)
    return high, (a - high.astype(F32)).astype(BF16)


def dot(a, b):
    return lax.dot_general(a, b, (((1,), (0,)), ((), ())), preferred_element_type=F32)


def product(a, b):
    a_high, a_low = split(a)
    b_high, b_low = split(b)
    return dot(a_high, b_high) + (dot(a_high, b_low) + dot(a_low, b_high))


def call(kernel, shapes, args, after=(), scratch=()):
    vmem = pl.BlockSpec(memory_space=pltpu.VMEM)
    smem = pl.BlockSpec(memory_space=pltpu.SMEM)

    def body(*refs):
        kernel(*refs[: len(args)], *refs[len(args) + len(after) :])

    return pl.pallas_call(
        body,
        out_shape=[jax.ShapeDtypeStruct(s, F32) for s in shapes],
        in_specs=[smem if a.dtype == jnp.int32 else vmem for a in args] + [pl.BlockSpec(memory_space=pl.ANY)] * len(after),
        out_specs=[vmem] * len(shapes),
        scratch_shapes=[pltpu.VMEM(s, F32) for s in scratch],
        compiler_params=pltpu.CompilerParams(vmem_limit_bytes=VMEM_LIMIT),
        name=kernel.__name__,
    )(*args, *after)


def copy_out(copies_ref, block):
    for i in range(copies_ref.shape[0]):
        copies_ref[i] = block


def begin(across_ref, copies_ref):
    half = across_ref.shape[0] // 2
    copy_out(copies_ref, jnp.concatenate([across_ref[:half, :], across_ref[half:, :]], axis=1))


def join(rows_b_ref, rows_a_ref, own_ref):
    lines = rows_b_ref.shape[0]
    own_ref[:lines, :] = rows_b_ref[...]
    own_ref[lines:, :] = rows_a_ref[...]


def send(block_ref, copies_ref):
    copy_out(copies_ref, block_ref[...])


def merge(core, same, other, whole_ref):
    whole_ref[:, pl.ds(core, 1)] = same[...][:, None]
    whole_ref[:, pl.ds(1 - core, 1)] = other[...][:, None]
    chips, cores, shard, width = whole_ref.shape
    return whole_ref[...].reshape(chips * cores * shard, width)


def solve(core_ref, inverse_ref, same_ref, other_ref, x_ref, copies_ref, whole_ref):
    x = product(inverse_ref[...], merge(core_ref[0], same_ref, other_ref, whole_ref))
    x_ref[...] = x
    copy_out(copies_ref, x)


def couple(core_ref, rhs_ref, across_ref, same_ref, other_ref, copies_ref, whole_ref):
    planes, _, lanes = across_ref.shape
    lines = lanes // 2
    parts = [across_ref[z] for z in range(planes)]
    parts = [jnp.concatenate([p[:, :lines], p[:, lines:]], axis=0) for p in parts]
    x = merge(core_ref[0], same_ref, other_ref, whole_ref)
    copy_out(copies_ref, rhs_ref[...] - product(jnp.concatenate(parts, axis=1), x))


def gather_x(refs, place, core, out_ref, at):
    for same, other in refs:
        shard = same.shape[-2]
        out_ref[pl.ds(pl.multiple_of(at + core * shard, shard), shard), :] = same[place]
        out_ref[pl.ds(pl.multiple_of(at + (1 - core) * shard, shard), shard), :] = other[place]
        at += 2 * shard


def near_kernel(planes, offsets, plane_ref, core_ref, b_same, b_other, a_same, a_other, *refs):
    count = len(offsets)
    row_refs, (total_ref, x_ref, rows_ref, semaphores) = refs[:count], refs[count:]
    block = rows_ref.shape[1]
    copies = [pltpu.make_async_copy(r, rows_ref.at[n], semaphores.at[n]) for n, r in enumerate(row_refs)]
    for copy in copies:
        copy.start()
    for n, offset in enumerate(offsets):
        place = lax.rem(plane_ref[0] + offset, planes)
        gather_x(((b_same, b_other), (a_same, a_other)), place, core_ref[0], x_ref, n * block)
    for n in range(0, count, 2):
        last = min(n + 2, count)
        for copy in copies[n:last]:
            copy.wait()
        rows = rows_ref[n:last].reshape((last - n) * block, rows_ref.shape[2])
        part = product(x_ref[n * block : last * block].T, rows)
        total_ref[...] = part if n == 0 else total_ref[...] + part


def update_near(plane, core, x, blocks, offsets, planes):
    height, width = blocks[0].shape[1], x[0].shape[2]
    vmem, smem = pl.BlockSpec(memory_space=pltpu.VMEM), pl.BlockSpec(memory_space=pltpu.SMEM)
    count, block = len(blocks), blocks[0].shape[0]
    return pl.pallas_call(
        functools.partial(near_kernel, planes, offsets),
        out_shape=jax.ShapeDtypeStruct((width, height), F32),
        in_specs=[smem] * 2 + [vmem] * len(x) + [pl.BlockSpec(memory_space=pl.ANY)] * count,
        out_specs=vmem,
        scratch_shapes=[
            pltpu.VMEM((count * block, width), F32),
            pltpu.VMEM((count, block, height), F32),
            pltpu.SemaphoreType.DMA((count,)),
        ],
        compiler_params=pltpu.CompilerParams(vmem_limit_bytes=UPDATE_LIMIT),
        name="update_near",
    )(plane, core, *x, *blocks)


def far_kernel(planes, plane_ref, core_ref, *refs):
    x_refs, rhs_in, total_in, row_refs = refs[:4], refs[4], refs[5], refs[6:-7]
    out_ref, parts_ref, x_ref, rhs_ref, total_ref, rows_ref, semaphores = refs[-7:]
    place = lax.rem(plane_ref[0] + planes // 2, planes)
    lines = row_refs[0].shape[0]
    pairs = [(r.at[pl.ds(place, 1)], parts_ref.at[pl.ds(n, 1)]) for n, r in enumerate(x_refs)]
    pairs += [(r, rows_ref.at[pl.ds(n * lines, lines)]) for n, r in enumerate(row_refs)] + [(total_in, total_ref), (rhs_in, rhs_ref)]
    copies = [pltpu.make_async_copy(*pair, semaphores.at[n]) for n, pair in enumerate(pairs)]
    for copy in copies:
        copy.start()
    for copy in copies[:-2]:
        copy.wait()
    parts = [parts_ref.at[pl.ds(n, 1)] for n in range(4)]
    gather_x((parts[:2], parts[2:]), 0, core_ref[0], x_ref, 0)
    part = product(x_ref[...].T, rows_ref[...])
    copies[-2].wait()
    part = (part + total_ref[...]).T
    copies[-1].wait()
    out_ref[...] = rhs_ref[...] - part


def update_far(plane, core, x, rhs, total, blocks, planes):
    vmem, smem, whole = (pl.BlockSpec(memory_space=m) for m in (pltpu.VMEM, pltpu.SMEM, pl.ANY))
    height, width = rhs.shape
    depth = sum(b.shape[0] for b in blocks)
    return pl.pallas_call(
        functools.partial(far_kernel, planes),
        out_shape=jax.ShapeDtypeStruct(rhs.shape, F32),
        in_specs=[smem] * 2 + [whole] * (len(x) + 2 + len(blocks)),
        out_specs=vmem,
        scratch_shapes=[
            pltpu.VMEM((len(x),) + x[0].shape[1:], F32),
            pltpu.VMEM((depth, width), F32),
            pltpu.VMEM(rhs.shape, F32),
            pltpu.VMEM(total.shape, F32),
            pltpu.VMEM((depth, height), F32),
            pltpu.SemaphoreType.DMA((len(x) + len(blocks) + 2,)),
        ],
        compiler_params=pltpu.CompilerParams(vmem_limit_bytes=UPDATE_LIMIT),
        name="update_far",
    )(plane, core, *x, rhs, total, *blocks)


def exchange(copies, axis):
    return lax.all_to_all(copies, axis, 0, 0, tiled=True)


def spread(copies):
    same = exchange(copies, "chip")
    return same, lax.ppermute(same, "core", [(0, 1), (1, 0)])


def ring(own, planes):
    def move(block, by):
        return lax.ppermute(block, "row", [(i, (i + by) % planes) for i in range(planes)])

    up = down = own
    blocks, offsets = [own], [0]
    half = planes // 2
    for step in range(1, half):
        up, down = move(up, 1), move(down, -1)
        blocks += [up, down]
        offsets += [planes - step, step]
    middle = own.shape[0] // 2
    blocks += [move(up[:middle], 1), move(down[middle:], -1)]
    offsets += [half]
    return blocks, tuple(offsets)


def make(planes, chips):
    def shards(rhs_above, rhs_a, rhs_b, rows_a_above, rows_b_above, rows_b_a, inverse_a, inverse_b):
        shard, width = rhs_b.shape
        lines, height = rows_b_above.shape
        plane, core = (lax.axis_index(a).astype(jnp.int32).reshape(1) for a in ("row", "core"))
        local, copies, whole = (shard, width), (chips, shard, width), (chips, 2, shard, width)

        (across_copies,) = call(begin, [(planes, shard // 2, 2 * lines)], [rows_b_a.T])
        across = exchange(across_copies, "row")
        (own,) = call(join, [(2 * lines, height)], [rows_b_above, rows_a_above])
        blocks, offsets = ring(own, planes)
        (rhs_copies,) = call(send, [copies], [rhs_b])
        x_b, x_copies = call(
            solve, [local, copies], [core, inverse_b.T, *spread(rhs_copies)], after=blocks[1:2] + [across], scratch=[whole]
        )
        x_b_all = spread(x_copies)
        (coupled,) = call(
            couple, [copies], [core, rhs_a, across, *x_b_all], after=blocks[5:6], scratch=[whole]
        )
        x_a, x_copies = call(
            solve, [local, copies], [core, inverse_a.T, *spread(coupled)], after=blocks[9:10], scratch=[whole]
        )
        x = x_b_all + spread(x_copies)
        total = update_near(plane, core, x, blocks[:-2], offsets[:-1], planes)
        return x_b, x_a, update_far(plane, core, x, rhs_above, total, blocks[-2:], planes)

    return shards


def solution(mesh):
    planes, columns = mesh.shape["row"], mesh.shape["col"]
    mesh = jax.sharding.Mesh(mesh.devices.reshape(planes, columns // 2, 2), ("row", "chip", "core"))
    column = ("chip", "core")
    in_specs = (
        P(column, "row"),
        P(column, "row"),
        P(column, "row"),
        P("row", column),
        P("row", column),
        P("row", column),
        P(None, column),
        P(None, column),
    )
    out_specs = (P(column, "row"), P(column, "row"), P(column, "row"))
    return jax.shard_map(
        make(planes, columns // 2), mesh=mesh, in_specs=in_specs, out_specs=out_specs, check_vma=False
    )
```
